32 devices in a mesh: row: 4 (over y, x), col: 8 (over z, core).
Axes of the slice: x: 2, y: 2, z: 4, core: 2. Of those that a mesh axis runs over, the one named last changes fastest.
Arguments:
- hidden_in: bfloat16 [8192, 14336], P(('row', 'col')), may hold values from -6 to 6
- out_grad: bfloat16 [8192, 4096], P(('row', 'col')), may hold values from -6 to 6
- proj_in: bfloat16 [14336, 128], replicated, may hold values from -0.046875 to 0.046875
- proj_out: bfloat16 [4096, 128], replicated, may hold values from -0.09375 to 0.09375
- inverse_fisher: float32 [16384, 16384], P('row', 'col'), may hold values from -0.0625 to 0.0625
- queries: float32 [16384, 256], P('col'), may hold values from -6 to 6
- lengths: int32 [64], replicated, may hold values from 32 to 4352, as said below
- offsets: int32 [64], replicated, may hold values from 0 to 8191, as said below
Outputs:
- scores: float32 [64, 256], P(('row', 'col'))
The draws below stay inside these ranges and needn't reach their ends.
Inputs may be any that keep to these rules, and one draw needn't show every extreme that they name: `lengths`: every sample has 32 tokens or more, and one sample has exactly 32; one sample has exactly half of all slots plus 256, and that is the most. Samples follow one another in slot order, each after 0 to 3 unused slots; slots after the last sample are unused; offsets[s] + lengths[s] <= 8192.
All inputs are finite; a program needn't handle non-finite values.
Results may differ from the reference program's by a relative error of at most 0.0003.
Values sent between devices are 32-bit elements; how exact they have to be, the bound alone decides.
No kernel may reach another device: no remote copies, remote signals or barrier semaphores. Data moves between devices by JAX's collectives and lax.ppermute only.
A program may use at most 128 MiB of HBM per device.

```python
import jax
import jax.numpy as jnp
from jax import lax

D = 4096
FF = 14336
RANK = 128
QUERIES = 256
LMIN = 32
TOK_DEV = 256
GRAD = 16384
TOKENS = 8192
SAMPLES = 64


def sample_layout(key):
    base = jax.random.fold_in(key, 7)
    key_weights = jax.random.fold_in(base, 1)
    key_pick = jax.random.fold_in(base, 2)
    key_gaps = jax.random.fold_in(base, 3)
    index_list = jnp.arange(SAMPLES, dtype=jnp.int32)
    longest = TOKENS // 2 + TOK_DEV
    weights = jax.random.randint(key_weights, (SAMPLES,), 1, 65).astype(jnp.int32)
    chosen = jax.random.randint(key_pick, (), 1, SAMPLES).astype(jnp.int32)
    weights = jnp.where((index_list == chosen) | (index_list == 0), 0, weights).astype(jnp.int32)
    gaps = jax.random.randint(key_gaps, (SAMPLES,), 0, 4).astype(jnp.int32)
    slack = TOKENS - longest - (SAMPLES - 1) * LMIN - jnp.sum(gaps)
    extra = weights * slack // jnp.sum(weights)
    lengths = jnp.where(index_list == 0, longest, LMIN + extra).astype(jnp.int32)
    sample_ends = jnp.cumsum(gaps + lengths).astype(jnp.int32)
    offsets = (sample_ends - lengths).astype(jnp.int32)
    return (lengths, offsets)


def draw_lengths(key, part):
    return sample_layout(key)[0]


def draw_offsets(key, part):
    return sample_layout(key)[1]


def with_spikes(result, stream_key, source, target, parts, factor):
    owner, partner = [(jnp.arange(result.shape[axis_at]) // (result.shape[axis_at] // parts)).reshape([-1 if axis == axis_at else 1 for axis in range(result.ndim)]) for axis_at in (source, target)]
    chosen = jax.random.permutation(stream_key, parts)[partner]
    strong = (owner == chosen) | (owner == (partner + parts // 2) % parts)
    return jnp.where(strong, factor * result, result)


def level_of(key, extent, cuts, least, largest):
    def one(dim, parts):
        draws = jax.random.uniform(jax.random.fold_in(jax.random.fold_in(key, 6), dim), (parts,), jnp.float32, least / len(cuts), largest / len(cuts))
        return jnp.repeat(jnp.exp(draws), extent[dim] // parts).reshape((-1,) + (1,) * (len(extent) - dim - 1))

    gain = one(*cuts[0])
    for cut in cuts[1:]:
        gain = gain * one(*cut)
    return gain


def centred(own_key, dims, scale, bound, pieces=(), held_as=jnp.bfloat16):
    drawn = jax.random.normal(own_key, dims, jnp.float32) * scale
    if len(pieces) > 0:
        drawn = level_of(own_key, dims, pieces, -0.22, 0.18) * drawn
    return jnp.clip(drawn, min=-bound, max=bound).astype(held_as)


def noise_with(rng, dims, deviation, most, shards, heavy, kind=jnp.bfloat16):
    values = deviation * jax.random.normal(rng, dims, jnp.float32)
    if shards:
        values = values * level_of(rng, dims, shards, -0.22, 0.18)
    return jnp.clip(with_spikes(values, jax.random.fold_in(rng, 3), *heavy), -most, most).astype(kind)


def setup_inputs(seed: int = 0) -> dict:
    splits = jax.random.split(jax.random.key(seed), 9)
    hidden_in = centred(splits[0], (TOKENS, FF), 1.0, 6.0, ((0, 32),))
    out_grad = centred(splits[1], (TOKENS, D), 1.0, 6.0, ((0, 32),))
    proj_in = centred(splits[2], (FF, RANK), FF ** -0.5, 0.046875)
    proj_out = centred(splits[3], (D, RANK), D ** -0.5, 0.09375)
    inverse_fisher = noise_with(splits[4], (GRAD, GRAD), GRAD ** -0.5, 0.0625, ((0, 4), (1, 8)), (1, 0, 8, 2.0), jnp.float32)
    queries = centred(splits[5], (GRAD, QUERIES), 1.0, 6.0, ((0, 8),), jnp.float32)
    lengths = draw_lengths(jax.random.fold_in(splits[8], 71), 0)
    offsets = draw_offsets(jax.random.fold_in(splits[8], 71), 0)
    return dict(hidden_in=hidden_in, out_grad=out_grad, proj_in=proj_in, proj_out=proj_out, inverse_fisher=inverse_fisher, queries=queries, lengths=lengths, offsets=offsets)


score_scale = 0.0625


def reference(hidden_in, out_grad, proj_in, proj_out, inverse_fisher, queries, lengths, offsets):
    proj_tokens = jnp.dot(hidden_in, proj_in, preferred_element_type=jnp.float32)
    proj_grads = jnp.dot(out_grad, proj_out, preferred_element_type=jnp.float32)
    sample_ends = offsets + lengths
    token_block = TOK_DEV
    block_count = TOKENS // token_block

    def scan_block(running, block_id):
        begin_row = (block_id * token_block).astype(jnp.int32)
        tokens_here = lax.dynamic_slice_in_dim(proj_tokens, begin_row, token_block, 0)
        grads_here = lax.dynamic_slice_in_dim(proj_grads, begin_row, token_block, 0)
        positions = begin_row + jnp.arange(token_block, dtype=jnp.int32)
        sample_id = jnp.sum((offsets[None, :] <= positions[:, None]).astype(jnp.int32), axis=1) - 1
        safe_id = jnp.clip(sample_id, 0, SAMPLES - 1).astype(jnp.int32)
        is_live = (sample_id >= 0) & (positions < sample_ends[safe_id])
        outer_terms = (grads_here[:, :, None] * tokens_here[:, None, :]).reshape(token_block, GRAD)
        outer_terms = outer_terms * is_live.astype(jnp.float32)[:, None]
        return running + jax.ops.segment_sum(outer_terms, safe_id, SAMPLES), None

    sample_grads, unused = lax.scan(scan_block, jnp.zeros((SAMPLES, GRAD), jnp.float32), jnp.arange(block_count, dtype=jnp.int32))
    precond = jnp.dot(inverse_fisher, queries, precision=lax.Precision.HIGHEST, preferred_element_type=jnp.float32)
    raw_scores = jnp.dot(sample_grads, precond, precision=lax.Precision.HIGHEST, preferred_element_type=jnp.float32)
    return score_scale * raw_scores / lengths.astype(jnp.float32)[:, None]
```

```python
import jax
import jax.numpy as jnp
from jax import lax
from jax.sharding import PartitionSpec as P

SHORTEST = 32
CORES = 2


score_scale = 0.0625


def near_dot(left, right):
    return jnp.dot(left, right, precision=lax.Precision.HIGH, preferred_element_type=jnp.float32)


def body(hidden_in, out_grad, proj_in, proj_out, inverse_fisher, queries, lengths, offsets):
    row_count = lax.axis_size("row")
    col_count = lax.axis_size("col")
    chip_count = col_count // CORES
    row_id = lax.axis_index("row")
    col_id = lax.axis_index("col")
    core_id = col_id % CORES
    chip_id = col_id // CORES
    device_id = row_id * col_count + col_id
    tok_rows = hidden_in.shape[0]
    rank = proj_out.shape[1]
    samples = lengths.shape[0]
    sample_ends = offsets + lengths
    window = min(samples, CORES * tok_rows // SHORTEST + 1)

    def other_core(x):
        return lax.ppermute(x, "col", [(i, i ^ 1) for i in range(col_count)])

    def along_row(x, step):
        return lax.ppermute(x, "row", [(i, i ^ step) for i in range(row_count)])

    def along_col(x, step):
        return lax.ppermute(x, "col", [(i, i ^ (CORES * step)) for i in range(col_count)])

    proj_grads = jnp.dot(out_grad, proj_out, preferred_element_type=jnp.float32)
    band = rank // row_count // CORES
    bands = proj_grads.reshape(tok_rows, row_count, CORES, band)
    grads_own = lax.dynamic_index_in_dim(bands, core_id, 2, False).reshape(tok_rows, row_count * band)
    grads_give = lax.dynamic_index_in_dim(bands, 1 - core_id, 2, False).reshape(tok_rows, row_count * band)
    proj_tokens = jnp.dot(hidden_in, proj_in, preferred_element_type=jnp.float32)
    grads_got = other_core(grads_give)
    tokens_got = other_core(proj_tokens)
    grads = jnp.concatenate([grads_own, grads_got])
    tokens = jnp.concatenate([proj_tokens, tokens_got])

    def window_start(chip):
        first_slot = chip * (CORES * tok_rows)
        passed = jnp.sum((sample_ends <= first_slot).astype(jnp.int32))
        return jnp.minimum(passed, samples - window)

    first_sample = window_start(device_id // CORES)
    win_offsets = lax.dynamic_slice_in_dim(offsets, first_sample, window, 0)
    win_ends = lax.dynamic_slice_in_dim(sample_ends, first_sample, window, 0)
    positions = jnp.concatenate(
        [d * tok_rows + jnp.arange(tok_rows, dtype=jnp.int32) for d in (device_id, device_id ^ 1)]
    )
    member = (
        (positions[None, :] >= win_offsets[:, None]) & (positions[None, :] < win_ends[:, None])
    ).astype(jnp.float32)
    weighted = member[:, None, :] * grads.T[None, :, :]
    wide = window * row_count * band
    window_grads = near_dot(weighted.reshape(wide, CORES * tok_rows), tokens)
    window_grads = window_grads.reshape(window, row_count, band * rank)

    sample_axis = jnp.arange(samples, dtype=jnp.int32)
    pieces, targets = [], []
    for step in range(row_count):
        peer = row_id ^ step
        piece = lax.dynamic_index_in_dim(window_grads, peer, 1, False)
        pieces.append(piece if step == 0 else along_row(piece, step))
        targets.append(window_start(peer * chip_count + chip_id) + jnp.arange(window, dtype=jnp.int32))
    onehot = (sample_axis[:, None] == jnp.concatenate(targets)[None, :]).astype(jnp.float32)
    sums = near_dot(onehot, jnp.concatenate(pieces))

    sums = sums.reshape(samples, chip_count, -1)
    own = lax.dynamic_index_in_dim(sums, chip_id, 1, False)
    for step in range(1, chip_count):
        own = own + along_col(lax.dynamic_index_in_dim(sums, chip_id ^ step, 1, False), step)
    parts = [own] + [along_col(own, step) for step in range(1, chip_count)]

    half = inverse_fisher.shape[0] // CORES
    give = near_dot(lax.dynamic_slice_in_dim(inverse_fisher, (1 - core_id) * half, half, 0), queries)
    got = other_core(give)
    keep = near_dot(lax.dynamic_slice_in_dim(inverse_fisher, core_id * half, half, 0), queries)
    product = (keep + got).reshape(chip_count, half // chip_count, -1)

    score_terms = jnp.zeros((samples, queries.shape[1]), jnp.float32)
    for step in range(chip_count):
        score_terms = score_terms + near_dot(parts[step], lax.dynamic_index_in_dim(product, chip_id ^ step, 0, False))

    everyone = ("row", "col")
    devices = row_count * col_count
    terms = lax.all_to_all(score_terms, everyone, split_axis=0, concat_axis=0, tiled=True)
    owned_rows = samples // devices
    owned_scores = jnp.sum(terms.reshape(devices, owned_rows, -1), axis=0)
    owned_lengths = lax.dynamic_slice_in_dim(lengths, device_id * owned_rows, owned_rows, 0)
    return score_scale * owned_scores / owned_lengths.astype(jnp.float32)[:, None]


def solution(mesh):
    in_specs = (
        P(("row", "col"), None),
        P(("row", "col"), None),
        P(),
        P(),
        P("row", "col"),
        P("col", None),
        P(),
        P(),
    )
    out_specs = P(("row", "col"), None)
    return jax.shard_map(body, mesh=mesh, in_specs=in_specs, out_specs=out_specs, check_vma=False)
```

```python
import functools

import jax
import jax.numpy as jnp
from jax import lax
from jax.experimental import pallas as pl
from jax.experimental.pallas import tpu as pltpu
from jax.sharding import PartitionSpec as P

SHORTEST = 32
STEP = 256
SPLIT = 512
CORES = 2
VMEM = pl.BlockSpec(memory_space=pltpu.VMEM)
SMEM = pl.BlockSpec(memory_space=pltpu.SMEM)
ANY = pl.BlockSpec(memory_space=pl.ANY)
HBM = pl.BlockSpec(memory_space=pltpu.HBM)

score_scale = 0.0625


def halves(x):
    high = x.astype(jnp.bfloat16)
    low = (x - high.astype(jnp.float32)).astype(jnp.bfloat16)
    return high, low


def dot(left, right):
    return jnp.dot(left, right, preferred_element_type=jnp.float32)


def params(mib):
    return pltpu.CompilerParams(vmem_limit_bytes=mib * 2**20)


def project_kernel(steps, row_count, place, hidden, grad, proj_in, proj_out, own, give, *scratch):
    hidden_v, grad_v, in_v, out_v, sems = scratch
    jobs = []
    for source, weights, left, right, count in (
        (grad, proj_out, grad_v, out_v, steps[0]),
        (hidden, proj_in, hidden_v, in_v, steps[1]),
    ):
        wide = source.shape[1] // count
        job = []
        for i in range(count):
            span = pl.ds(i * wide, wide)
            slot = len(jobs) * steps[0] + i
            a = pltpu.make_async_copy(source.at[:, span], left.at[:, span], sems.at[0, slot])
            b = pltpu.make_async_copy(weights.at[span, :], right.at[span, :], sems.at[1, slot])
            a.start()
            b.start()
            job.append((span, a, b))
        jobs.append((left, right, job))
    results = []
    for left, right, job in jobs:
        total = None
        for span, a, b in job:
            a.wait()
            b.wait()
            term = dot(left[:, span], right[span, :])
            total = term if total is None else total + term
        results.append(total)
    grads, tokens = results
    tok_rows, rank = tokens.shape
    band = rank // row_count // CORES
    turned = grads.T.reshape(row_count, CORES, band, tok_rows)
    first = turned[:, 0].reshape(row_count * band, tok_rows)
    second = turned[:, 1].reshape(row_count * band, tok_rows)
    mine = place[1] % CORES == 0
    tall = row_count * band
    for ref, value in ((own, jnp.where(mine, first, second)), (give, jnp.where(mine, second, first))):
        for i in range(tok_rows // rank):
            ref[i * tall : (i + 1) * tall, :] = value[:, i * rank : (i + 1) * rank]
        ref[tok_rows // rank * tall :, :] = tokens


def project(place, hidden_in, out_grad, proj_in, proj_out, row_count):
    tok_rows, rank = hidden_in.shape[0], proj_in.shape[1]
    steps = (2, 7)
    tall = tok_rows // rank * (rank // CORES) + tok_rows
    out = jax.ShapeDtypeStruct((tall, rank), jnp.float32)
    return pl.pallas_call(
        functools.partial(project_kernel, steps, row_count),
        out_shape=(out, out),
        in_specs=[SMEM, HBM, HBM, HBM, HBM],
        out_specs=(VMEM, VMEM),
        scratch_shapes=[
            pltpu.VMEM(hidden_in.shape, hidden_in.dtype),
            pltpu.VMEM(out_grad.shape, out_grad.dtype),
            pltpu.VMEM(proj_in.shape, proj_in.dtype),
            pltpu.VMEM(proj_out.shape, proj_out.dtype),
            pltpu.SemaphoreType.DMA((2, sum(steps))),
        ],
        compiler_params=params(53),
        name="project",
    )(place, hidden_in, out_grad, proj_in, proj_out)


def first_of_window(ends, first_slot, samples, window):
    passed = jnp.sum((ends[...] <= first_slot).astype(jnp.int32))
    return jnp.minimum(passed, samples - window)


def window_kernel(window, sizes, tok_rows, place, offsets, lengths, ends, own, got, *refs):
    row_count, col_count = sizes
    outs, left = refs[:row_count], refs[row_count]
    device = place[0] * col_count + place[1]
    first_sample = first_of_window(ends, device // CORES * (CORES * tok_rows), lengths.shape[0], window)
    rank = own.shape[1]
    strips = tok_rows // rank
    tall = (own.shape[0] - tok_rows) // strips
    pieces = [ref[i * tall : (i + 1) * tall, :] for ref in (own, got) for i in range(strips)]
    grads_high, grads_low = halves(jnp.concatenate(pieces, axis=1))
    high, low = halves(jnp.concatenate([own[strips * tall :, :], got[strips * tall :, :]], axis=0))
    tokens = jnp.concatenate([high, low], axis=1)
    lanes = lax.broadcasted_iota(jnp.int32, (1, 2 * tok_rows), 1)
    other = device + 1 - 2 * (place[1] % CORES)
    positions = jnp.where(lanes < tok_rows, device * tok_rows + lanes, (other - 1) * tok_rows + lanes)
    both = jnp.concatenate([grads_high, grads_low], axis=0)
    for w in range(window):
        begin = offsets[first_sample + w]
        inside = (positions >= begin) & (positions < begin + lengths[first_sample + w])
        left[w * 2 * tall : (w + 1) * 2 * tall, :] = both * inside.astype(jnp.bfloat16)
    sums = dot(left[...], tokens)
    band = tall // row_count
    sums = sums.reshape(window, 2, row_count, band, 2 * rank)
    sums = sums[:, 0, :, :, :rank] + (sums[:, 0, :, :, rank:] + sums[:, 1, :, :, :rank])
    for r in range(row_count):
        step = place[0] ^ r
        for s in range(row_count):

            @pl.when(step == s)
            def _():
                outs[s][...] = sums[:, r]


def windows(place, offsets, lengths, ends, own, got, window, sizes, tok_rows):
    rank = own.shape[1]
    tall = (own.shape[0] - tok_rows) // (tok_rows // rank)
    out = jax.ShapeDtypeStruct((window, tall // sizes[0], rank), jnp.float32)
    return pl.pallas_call(
        functools.partial(window_kernel, window, sizes, tok_rows),
        out_shape=(out,) * sizes[0],
        in_specs=[SMEM, SMEM, SMEM, VMEM, VMEM, VMEM],
        out_specs=(VMEM,) * sizes[0],
        scratch_shapes=[pltpu.VMEM((window * 2 * tall, 2 * tok_rows), jnp.bfloat16)],
        compiler_params=params(40),
        cost_estimate=pl.CostEstimate(
            flops=16 * window * tall * tok_rows * rank, bytes_accessed=8 * window * tall * rank, transcendentals=0
        ),
        name="windows",
    )(place, offsets, lengths, ends, own, got)


def spread_kernel(sizes, tok_rows, place, ends, *refs):
    row_count, col_count = sizes
    pieces, outs, total = refs[:row_count], refs[row_count + 1 : -1], refs[-1]
    total[...] = jnp.zeros_like(total)
    window = pieces[0].shape[0]
    chip = place[1] // CORES
    for d in range(row_count):
        source = (place[0] ^ d) * (col_count // CORES) + chip
        first = first_of_window(ends, source * (CORES * tok_rows), total.shape[0], window)
        span = pl.ds(first, window)
        total[span] = total[span] + pieces[d][...]
    count = outs[0].shape[0]
    for d, out in enumerate(outs):
        out[...] = total[pl.ds((chip ^ d) * count, count)]


def spread(place, ends, pieces, after, samples, sizes, tok_rows):
    tail = pieces[0].shape[1:]
    chip_count = sizes[1] // CORES
    out = jax.ShapeDtypeStruct((samples // chip_count, *tail), jnp.float32)
    return pl.pallas_call(
        functools.partial(spread_kernel, sizes, tok_rows),
        out_shape=(out,) * chip_count,
        in_specs=[SMEM, VMEM] + [VMEM] * len(pieces) + [ANY],
        out_specs=(VMEM,) * chip_count,
        scratch_shapes=[pltpu.VMEM((samples, *tail), jnp.float32)],
        compiler_params=params(40),
        name="spread",
    )(place, ends, *pieces, after)


def sum_kernel(after, through, *refs):
    total = refs[0][...]
    for ref in refs[1:-2]:
        total = total + ref[...]
    refs[-2][...] = total


def sum_of(parts, after, through):
    return pl.pallas_call(
        sum_kernel,
        out_shape=(
            jax.ShapeDtypeStruct(parts[0].shape, jnp.float32),
            jax.ShapeDtypeStruct(through.shape, through.dtype),
        ),
        in_specs=[ANY, ANY] + [VMEM] * len(parts),
        out_specs=(VMEM, ANY),
        input_output_aliases={1: 1},
        compiler_params=params(40),
        name="sum_parts",
    )(after, through, *parts)


def across(left, right):
    return lax.dot_general(left, right, (((1,), (1,)), ((), ())), preferred_element_type=jnp.float32)


def product_kernel(chunks, turn, half, place, after, fisher, queries, *refs):
    count = len(chunks) + (1 if turn else 0)
    outs, scratch = refs[:count], refs[count:]
    fisher_v, split, sems = scratch[:3]
    core = place[1] % CORES
    if turn:
        start = pltpu.make_async_copy(queries, scratch[3], sems.at[0])
        start.start()
    copies, at = [], 0
    for ours, first, rows in chunks:
        source = jnp.where(core == 0, first, half + first) if ours else jnp.where(core == 0, half + first, first)
        source = pl.multiple_of(source, STEP)
        for step in range(0, rows, STEP):
            copy = pltpu.make_async_copy(
                fisher.at[pl.ds(source + step, STEP), :],
                fisher_v.at[pl.ds(at, STEP), :],
                sems.at[1 + at // STEP],
            )
            copy.start()
            copies.append(copy)
            at += STEP
    if turn:
        start.wait()
        high, low = halves(scratch[3][...].T)
        width = high.shape[0]
        outs[0][:width, :] = high
        outs[0][width:, :] = low
        turned, outs = outs[0], outs[1:]
    else:
        turned = queries
        width = turned.shape[0] // 2
    at = 0
    for out, (_, _, rows) in zip(outs, chunks):
        for begin in range(0, rows, SPLIT):
            size = min(SPLIT, rows - begin)
            for step in range(0, size, STEP):
                copies[at // STEP].wait()
                split[0, step : step + STEP, :], split[1, step : step + STEP, :] = halves(fisher_v[at : at + STEP, :])
                at += STEP
            term = across(turned[...], split[0, :size, :])
            term = term[:width] + (term[width:] + across(turned[:width, :], split[1, :size, :]))
            out[:, begin : begin + size] = term


def product(place, after, inverse_fisher, queries, chunks, turn=False):
    width = queries.shape[1] if turn else queries.shape[0] // 2
    depth = inverse_fisher.shape[1]
    out_shape = [jax.ShapeDtypeStruct((2 * width, depth), jnp.bfloat16)] if turn else []
    out_shape += [jax.ShapeDtypeStruct((width, chunk[2]), jnp.float32) for chunk in chunks]
    rows = sum(chunk[2] for chunk in chunks)
    half = inverse_fisher.shape[0] // CORES
    return pl.pallas_call(
        functools.partial(product_kernel, chunks, turn, half),
        out_shape=tuple(out_shape),
        in_specs=[SMEM, ANY, HBM, ANY if turn else VMEM],
        out_specs=(VMEM,) * len(out_shape),
        scratch_shapes=[
            pltpu.VMEM((rows, depth), jnp.float32),
            pltpu.VMEM((2, min(SPLIT, max(chunk[2] for chunk in chunks)), depth), jnp.bfloat16),
            pltpu.SemaphoreType.DMA((1 + rows // STEP,)),
        ]
        + ([pltpu.VMEM(queries.shape, queries.dtype)] if turn else []),
        compiler_params=params(36),
        cost_estimate=pl.CostEstimate(
            flops=6 * rows * depth * width, bytes_accessed=4 * rows * depth, transcendentals=0
        ),
        name="product",
    )(place, after, inverse_fisher, queries)


def merge(keeps, gots):
    shape = (keeps[0].shape[0], sum(keep.shape[1] for keep in keeps))

    def kernel(*refs):
        ins, (high, low) = refs[:-2], refs[-2:]
        left = [(ref, at) for ref in ins[: len(keeps)] for at in range(0, ref.shape[1], STEP)]
        right = [(ref, at) for ref in ins[len(keeps) :] for at in range(0, ref.shape[1], STEP)]
        for i, ((a, at), (b, to)) in enumerate(zip(left, right)):
            span = slice(i * STEP, (i + 1) * STEP)
            high[:, span], low[:, span] = halves(a[:, at : at + STEP] + b[:, to : to + STEP])

    out = jax.ShapeDtypeStruct(shape, jnp.bfloat16)
    return pl.pallas_call(
        kernel,
        out_shape=(out, out),
        in_specs=[VMEM] * (len(keeps) + len(gots)),
        out_specs=(VMEM, VMEM),
        compiler_params=params(36),
        name="merge",
    )(*keeps, *gots)


def score_kernel(chip_count, pieces, band, place, *refs):
    parts, high, low = refs[:chip_count], refs[chip_count : chip_count + pieces], refs[chip_count + pieces : -2]
    out, left = refs[-2:]
    count = parts[0].shape[0] // band
    rank = parts[0].shape[1]
    chip = place[1] // CORES
    for d, part in enumerate(parts):
        rows = pl.ds(pl.multiple_of((chip ^ d) * count, count), count)
        for a in range(band):
            left[rows, a * rank : (a + 1) * rank] = part[pl.ds(a, count, stride=band), :]
    left_high, left_low = halves(left[...])
    samples = left_high.shape[0]
    both = jnp.concatenate([left_high, left_low], axis=0)
    total, at = None, 0
    for p in range(pieces):
        depth = high[p].shape[1]
        span = slice(at, at + depth)
        term = across(both[:, span], high[p][...])
        term = term[:samples] + (term[samples:] + across(left_high[:, span], low[p][...]))
        total = term if total is None else total + term
        at += depth
    out[...] = total.reshape(out.shape)


def score(place, parts, high, low, samples, devices, band):
    rank = parts[0].shape[1]
    width = high[0].shape[0]
    return pl.pallas_call(
        functools.partial(score_kernel, len(parts), len(high), band),
        out_shape=jax.ShapeDtypeStruct((devices, samples // devices, width), jnp.float32),
        in_specs=[SMEM] + [VMEM] * (len(parts) + len(high) + len(low)),
        out_specs=VMEM,
        scratch_shapes=[pltpu.VMEM((samples, band * rank), jnp.float32)],
        compiler_params=params(40),
        name="score",
    )(place, *parts, *high, *low)


def body(hidden_in, out_grad, proj_in, proj_out, inverse_fisher, queries, lengths, offsets):
    row_count = lax.axis_size("row")
    col_count = lax.axis_size("col")
    sizes = (row_count, col_count)
    chip_count = col_count // CORES
    row_id = lax.axis_index("row")
    col_id = lax.axis_index("col")
    tok_rows = hidden_in.shape[0]
    rank = proj_out.shape[1]
    samples = lengths.shape[0]
    ends = (offsets + lengths)[None, :]
    window = min(samples, CORES * tok_rows // SHORTEST + 1)
    band = rank // row_count // CORES
    place = jnp.stack([row_id, col_id])

    def other_core(x):
        return lax.ppermute(x, "col", [(i, i ^ 1) for i in range(col_count)])

    def along_row(x, step):
        return lax.ppermute(x, "row", [(i, i ^ step) for i in range(row_count)])

    def along_col(x, step):
        return lax.ppermute(x, "col", [(i, i ^ (CORES * step)) for i in range(col_count)])

    own, give = project(place, hidden_in, out_grad, proj_in, proj_out, row_count)
    got = other_core(give)
    pieces = windows(place, offsets, lengths, ends, own, got, window, sizes, tok_rows)

    half = inverse_fisher.shape[0] // CORES
    mid, quarter = half // 2, half // 4
    arrived = [pieces[0]] + [along_row(pieces[d], d) for d in reversed(range(1, row_count))][::-1]
    turned, give_a = product(place, pieces[0], inverse_fisher, queries, [(False, 0, mid)], turn=True)
    chunks = spread(place, ends, arrived, give_a, samples, sizes, tok_rows)

    arrived = [chunks[0]] + [along_col(chunks[d], d) for d in reversed(range(1, chip_count))][::-1]
    give_b, keep_a = product(place, chunks[0], inverse_fisher, turned, [(False, mid, mid), (True, 0, quarter)])
    total, give_b = sum_of(arrived[::-1], keep_a, give_b)

    parts = [total] + [along_col(total, d) for d in reversed(range(1, chip_count))][::-1]
    (keep_b,) = product(place, total, inverse_fisher, turned, [(True, quarter, half - quarter)])
    high, low = merge([keep_a, keep_b], [other_core(give_a), other_core(give_b)])
    parts = [part.reshape(-1, rank) for part in parts]
    devices = row_count * col_count
    score_terms = score(place, parts, [high], [low], samples, devices, band)

    terms = lax.all_to_all(score_terms, ("row", "col"), split_axis=0, concat_axis=0, tiled=True)
    owned_rows = samples // devices
    owned_scores = jnp.sum(terms, axis=0)
    device_id = row_id * col_count + col_id
    owned_lengths = lax.dynamic_slice_in_dim(lengths, device_id * owned_rows, owned_rows, 0)
    return score_scale * owned_scores / owned_lengths.astype(jnp.float32)[:, None]


def solution(mesh):
    in_specs = (
        P(("row", "col"), None),
        P(("row", "col"), None),
        P(),
        P(),
        P("row", "col"),
        P("col", None),
        P(),
        P(),
    )
    out_specs = P(("row", "col"), None)
    return jax.shard_map(body, mesh=mesh, in_specs=in_specs, out_specs=out_specs, check_vma=False)
```

```python
import functools

import jax
import jax.numpy as jnp
from jax import lax
from jax.experimental import pallas as pl
from jax.experimental.pallas import tpu as pltpu
from jax.sharding import PartitionSpec as P

SHORTEST = 32
STEP = 256
MOST, LATER = 1, 64
CORES = 2
VMEM = pl.BlockSpec(memory_space=pltpu.VMEM)
SMEM = pl.BlockSpec(memory_space=pltpu.SMEM)
ANY = pl.BlockSpec(memory_space=pl.ANY)
HBM = pl.BlockSpec(memory_space=pltpu.HBM)

score_scale = 0.0625


def halves(x):
    high = x.astype(jnp.bfloat16)
    low = (x - high.astype(jnp.float32)).astype(jnp.bfloat16)
    return high, low


def dot(left, right):
    return jnp.dot(left, right, preferred_element_type=jnp.float32)


def params(mib):
    return pltpu.CompilerParams(vmem_limit_bytes=mib * 2**20)


def project_kernel(steps, row_count, place, hidden, grad, proj_in, proj_out, own, give, *scratch):
    hidden_v, grad_v, in_v, out_v, sems = scratch
    jobs = []
    for source, weights, left, right, count in (
        (grad, proj_out, grad_v, out_v, steps[0]),
        (hidden, proj_in, hidden_v, in_v, steps[1]),
    ):
        wide = source.shape[1] // count
        job = []
        for i in range(count):
            span = pl.ds(i * wide, wide)
            slot = len(jobs) * steps[0] + i
            a = pltpu.make_async_copy(source.at[:, span], left.at[:, span], sems.at[0, slot])
            b = pltpu.make_async_copy(weights.at[span, :], right.at[span, :], sems.at[1, slot])
            a.start()
            b.start()
            job.append((span, a, b))
        jobs.append((left, right, job))
    results = []
    for left, right, job in jobs:
        total = None
        for span, a, b in job:
            a.wait()
            b.wait()
            term = dot(left[:, span], right[span, :])
            total = term if total is None else total + term
        results.append(total)
    grads, tokens = results
    tok_rows, rank = tokens.shape
    band = rank // row_count // CORES
    turned = grads.T.reshape(row_count, CORES, band, tok_rows)
    first = turned[:, 0].reshape(row_count * band, tok_rows)
    second = turned[:, 1].reshape(row_count * band, tok_rows)
    mine = place[1] % CORES == 0
    tall = row_count * band
    for ref, value in ((own, jnp.where(mine, first, second)), (give, jnp.where(mine, second, first))):
        for i in range(tok_rows // rank):
            ref[i * tall : (i + 1) * tall, :] = value[:, i * rank : (i + 1) * rank]
        ref[tok_rows // rank * tall :, :] = tokens


def project(place, hidden_in, out_grad, proj_in, proj_out, row_count):
    tok_rows, rank = hidden_in.shape[0], proj_in.shape[1]
    steps = (2, 7)
    tall = tok_rows // rank * (rank // CORES) + tok_rows
    out = jax.ShapeDtypeStruct((tall, rank), jnp.float32)
    return pl.pallas_call(
        functools.partial(project_kernel, steps, row_count),
        out_shape=(out, out),
        in_specs=[SMEM, HBM, HBM, HBM, HBM],
        out_specs=(VMEM, VMEM),
        scratch_shapes=[
            pltpu.VMEM(hidden_in.shape, hidden_in.dtype),
            pltpu.VMEM(out_grad.shape, out_grad.dtype),
            pltpu.VMEM(proj_in.shape, proj_in.dtype),
            pltpu.VMEM(proj_out.shape, proj_out.dtype),
            pltpu.SemaphoreType.DMA((2, sum(steps))),
        ],
        compiler_params=params(53),
        name="project",
    )(place, hidden_in, out_grad, proj_in, proj_out)


def prepare_kernel(sizes, slots, after, offsets, lengths, queries, table, most, turned):
    row_count, col_count = sizes
    chips = row_count * col_count // CORES
    begin = lax.broadcasted_iota(jnp.int32, (chips, offsets.shape[1]), 0) * slots
    ended = (offsets[...] + lengths[...] <= begin).astype(jnp.int32).sum(axis=1, keepdims=True)
    begun = (offsets[...] < begin + slots).astype(jnp.int32).sum(axis=1, keepdims=True)
    lanes = lax.broadcasted_iota(jnp.int32, (chips, 2 * LATER), 1)
    met = jnp.sum((begun - ended).reshape(row_count, chips // row_count, 1), axis=0)
    most[0] = jnp.max(met)
    table[...] = jnp.where(lanes < LATER, jnp.where(lanes == MOST, jnp.max(met), ended), begun)
    high, low = halves(queries[...].T)
    width = high.shape[0]
    turned[:width, :] = high
    turned[width:, :] = low


def prepare(after, offsets, lengths, queries, sizes, tok_rows):
    depth, width = queries.shape
    chips = sizes[0] * sizes[1] // CORES
    return pl.pallas_call(
        functools.partial(prepare_kernel, sizes, CORES * tok_rows),
        out_shape=(
            jax.ShapeDtypeStruct((chips, 2 * LATER), jnp.int32),
            jax.ShapeDtypeStruct((1,), jnp.int32),
            jax.ShapeDtypeStruct((2 * width, depth), jnp.bfloat16),
        ),
        in_specs=[ANY, VMEM, VMEM, VMEM],
        out_specs=(VMEM, SMEM, VMEM),
        compiler_params=params(16),
        cost_estimate=pl.CostEstimate(flops=depth * width * 2048, bytes_accessed=8 * depth * width, transcendentals=0),
        name="prepare",
    )(after, offsets[None, :], lengths[None, :], queries)


def window_kernel(window, sizes, tok_rows, place, offsets, lengths, table, own, got, *refs):
    row_count, col_count = sizes
    outs, left = refs[:row_count], refs[row_count]
    device = place[0] * col_count + place[1]
    first_sample = jnp.minimum(table[device // CORES, 0], lengths.shape[0] - window)
    rank = own.shape[1]
    strips = tok_rows // rank
    tall = (own.shape[0] - tok_rows) // strips
    pieces = [ref[i * tall : (i + 1) * tall, :] for ref in (own, got) for i in range(strips)]
    grads_high, grads_low = halves(jnp.concatenate(pieces, axis=1))
    high, low = halves(jnp.concatenate([own[strips * tall :, :], got[strips * tall :, :]], axis=0))
    tokens = jnp.concatenate([high, low], axis=1)
    lanes = lax.broadcasted_iota(jnp.int32, (1, 2 * tok_rows), 1)
    other = device + 1 - 2 * (place[1] % CORES)
    positions = jnp.where(lanes < tok_rows, device * tok_rows + lanes, (other - 1) * tok_rows + lanes)
    both = jnp.concatenate([grads_high, grads_low], axis=0)
    for w in range(window):
        begin = offsets[first_sample + w]
        inside = (positions >= begin) & (positions < begin + lengths[first_sample + w])
        left[w * 2 * tall : (w + 1) * 2 * tall, :] = both * inside.astype(jnp.bfloat16)
    sums = dot(left[...], tokens)
    band = tall // row_count
    sums = sums.reshape(window, 2, row_count, band, 2 * rank)
    sums = sums[:, 0, :, :, :rank] + (sums[:, 0, :, :, rank:] + sums[:, 1, :, :, :rank])
    for r in range(row_count):
        step = place[0] ^ r
        for s in range(row_count):

            @pl.when(step == s)
            def _():
                outs[s][...] = sums[:, r]


def windows(place, offsets, lengths, table, own, got, window, sizes, tok_rows):
    rank = own.shape[1]
    tall = (own.shape[0] - tok_rows) // (tok_rows // rank)
    out = jax.ShapeDtypeStruct((window, tall // sizes[0], rank), jnp.float32)
    return pl.pallas_call(
        functools.partial(window_kernel, window, sizes, tok_rows),
        out_shape=(out,) * sizes[0],
        in_specs=[SMEM, SMEM, SMEM, SMEM, VMEM, VMEM],
        out_specs=(VMEM,) * sizes[0],
        scratch_shapes=[pltpu.VMEM((window * 2 * tall, 2 * tok_rows), jnp.bfloat16)],
        compiler_params=params(34),
        cost_estimate=pl.CostEstimate(
            flops=16 * window * tall * tok_rows * rank, bytes_accessed=8 * window * tall * rank, transcendentals=0
        ),
        name="windows",
    )(place, offsets, lengths, table, own, got)


def runs(place, table, sizes, step, samples, window):
    row_count, col_count = sizes
    chip, base, found = (place[1] // CORES) ^ step, 0, []
    for d in range(row_count):
        at = (place[0] ^ d) * (col_count // CORES) + chip
        first = table[at, 0]
        count = jnp.minimum(table[at, LATER] - first, window)
        found.append((first, count, first - jnp.minimum(first, samples - window), base))
        base = base + count
    return found


def pack_kernel(sizes, samples, cap, place, table, *refs):
    pieces, (first, rest, total) = refs[: sizes[0]], refs[sizes[0] + 1 :]
    window, band, rank = pieces[0].shape
    total[...] = jnp.zeros_like(total)
    for piece, (_, count, skip, base) in zip(pieces, runs(place, table, sizes, 0, samples, window)):

        def move(i, carry):
            total[base + i] = piece[skip + i]
            return carry

        lax.fori_loop(0, count, move, 0)
    rows = total.reshape(total.shape[0] * band, rank)
    for a in range(band):
        first[a * cap : (a + 1) * cap, :] = rows[pl.ds(a, cap, stride=band), :]
    for k in range(rest.shape[0]):

        @pl.when(table[0, MOST] > (k + 1) * cap)
        def _():
            for a in range(band):
                rest[k, a * cap : (a + 1) * cap, :] = rows[pl.ds((k + 1) * cap * band + a, cap, stride=band), :]


def pack(place, table, pieces, after, samples, cap, sizes):
    window, band, rank = pieces[0].shape
    rounds = -(-len(pieces) * window // cap)
    return pl.pallas_call(
        functools.partial(pack_kernel, sizes, samples, cap),
        out_shape=(
            jax.ShapeDtypeStruct((band * cap, rank), jnp.float32),
            jax.ShapeDtypeStruct((max(rounds - 1, 1), band * cap, rank), jnp.float32),
        ),
        in_specs=[SMEM, SMEM] + [VMEM] * len(pieces) + [ANY],
        out_specs=(VMEM, VMEM),
        scratch_shapes=[pltpu.VMEM((max(rounds, 2) * cap, band, rank), jnp.float32)],
        compiler_params=params(16),
        name="pack",
    )(place, table, *pieces, after)


def release_kernel(*refs):
    pass


def release(parts, after):
    return pl.pallas_call(
        release_kernel,
        out_shape=tuple(jax.ShapeDtypeStruct(part.shape, part.dtype) for part in parts),
        in_specs=[ANY] * (len(parts) + 1),
        out_specs=(ANY,) * len(parts),
        input_output_aliases={i + 1: i for i in range(len(parts))},
        compiler_params=params(16),
        name="release",
    )(after, *parts)


def across(left, right):
    return lax.dot_general(left, right, (((1,), (1,)), ((), ())), preferred_element_type=jnp.float32)


def rows_from(core, chunk, half):
    ours, first, _ = chunk
    return pl.multiple_of(jnp.where((core == 0) == ours, first, half + first), STEP)


def product_kernel(chunks, later, half, place, after, fisher, turned, *refs):
    count = len(chunks) + (1 if later else 0)
    heads, outs, (fisher_v, split, sems) = refs[: -3 - count], refs[-3 - count : -3], refs[-3:]
    core = place[1] % CORES
    ready = heads[0].shape[0] if heads else 0
    width = turned.shape[0] // 2
    copies, at = [], 0
    for chunk in chunks:
        source = rows_from(core, chunk, half)
        for step in range(0, chunk[2], STEP):
            if at >= ready:
                copy = pltpu.make_async_copy(
                    fisher.at[pl.ds(source + step, STEP), :],
                    fisher_v.at[pl.ds(at - ready, STEP), :],
                    sems.at[1 + at // STEP],
                )
                copy.start()
                copies.append(copy)
            else:
                copies.append(None)
            at += STEP
    if later:
        coming, outs = outs[0], outs[1:]
        source = rows_from(core, later, half)
        ahead = pltpu.make_async_copy(fisher.at[pl.ds(source, coming.shape[0]), :], coming, sems.at[0])
        ahead.start()
    at = 0
    for out, (_, _, rows) in zip(outs, chunks):
        for begin in range(0, rows, split.shape[1]):
            size = min(split.shape[1], rows - begin)
            for step in range(0, size, STEP):
                if copies[at // STEP] is None:
                    piece = heads[0][at : at + STEP, :]
                else:
                    copies[at // STEP].wait()
                    piece = fisher_v[at - ready : at - ready + STEP, :]
                split[0, step : step + STEP, :], split[1, step : step + STEP, :] = halves(piece)
                at += STEP
            term = across(turned[...], split[0, :size, :])
            term = term[:width] + (term[width:] + across(turned[:width, :], split[1, :size, :]))
            span = slice(begin, begin + size)
            out[:width, span], out[width:, span] = halves(term)
    if later:
        ahead.wait()


def product(place, after, inverse_fisher, head, turned, chunks, later=None):
    width = turned.shape[0] // 2
    heads = [] if head is None else [head]
    depth = inverse_fisher.shape[1]
    out_shape = [jax.ShapeDtypeStruct((2 * STEP, depth), jnp.float32)] if later else []
    out_shape += [jax.ShapeDtypeStruct((2 * width, chunk[2]), jnp.bfloat16) for chunk in chunks]
    rows = sum(chunk[2] for chunk in chunks)
    half = inverse_fisher.shape[0] // CORES
    return pl.pallas_call(
        functools.partial(product_kernel, chunks, later, half),
        out_shape=tuple(out_shape),
        in_specs=[SMEM, ANY, HBM, VMEM] + [VMEM] * len(heads),
        out_specs=(VMEM,) * len(out_shape),
        scratch_shapes=[
            pltpu.VMEM((rows - sum(h.shape[0] for h in heads), depth), jnp.float32),
            pltpu.VMEM((2, 2 * STEP, depth), jnp.bfloat16),
            pltpu.SemaphoreType.DMA((1 + rows // STEP,)),
        ],
        compiler_params=params(34),
        cost_estimate=pl.CostEstimate(
            flops=6 * rows * depth * width, bytes_accessed=4 * rows * depth, transcendentals=0
        ),
        name="product",
    )(place, after, inverse_fisher, turned, *heads)


def rows_times(parts, products, left, cap):
    rank = parts[0].shape[1]
    for i, part in enumerate(parts):
        for a in range(part.shape[0] // cap):
            left[i * cap : (i + 1) * cap, a * rank : (a + 1) * rank] = part[a * cap : (a + 1) * cap, :]
    slots = left.shape[0]
    total, at = None, 0
    for ref in products:
        width, depth = ref.shape[0] // 2, ref.shape[1]
        high, low = halves(left[:, at : at + depth])
        term = across(jnp.concatenate([high, low], axis=0), ref[:width, :])
        term = term[:slots] + (term[slots:] + across(high, ref[width:, :]))
        total = term if total is None else total + term
        at += depth
    return total


def own_score_kernel(count, cap, *refs):
    refs[-2][...] = rows_times(refs[:count], refs[count:-2], refs[-1], cap)


def own_score(parts, products, cap):
    depth = parts[0].shape[0] // cap * parts[0].shape[1]
    rows, width = len(parts) * cap, products[0].shape[0] // 2
    return pl.pallas_call(
        functools.partial(own_score_kernel, len(parts), cap),
        out_shape=jax.ShapeDtypeStruct((rows, width), jnp.float32),
        in_specs=[VMEM] * (len(parts) + len(products)),
        out_specs=VMEM,
        scratch_shapes=[pltpu.VMEM((rows, depth), jnp.float32)],
        compiler_params=params(16),
        cost_estimate=pl.CostEstimate(
            flops=64 * rows * depth * width, bytes_accessed=4 * depth * width, transcendentals=0
        ),
        name="own_score",
    )(*parts, *products)


def score_kernel(sizes, samples, window, cap, place, table, turn, own, *refs):
    chip_count = sizes[1] // CORES
    out, left = refs[-2:]
    total = own[...] + rows_times(refs[:chip_count], refs[chip_count:-2], left, cap)
    slots = chip_count * cap
    lanes = lax.broadcasted_iota(jnp.int32, (1, slots), 1)
    held = jnp.full((1, slots), -1, jnp.int32)
    for step in range(chip_count):
        at = lanes - step * cap
        here = (at >= 0) & (at < cap)
        at = at + turn[0] * cap
        for first, count, _, base in runs(place, table, sizes, step, samples, window):
            held = jnp.where(here & (at >= base) & (at < base + count), first + at - base, held)
    hit = lax.broadcasted_iota(jnp.int32, (samples, slots), 0) == held
    chosen = hit.astype(jnp.bfloat16)
    high, low = halves(total)
    out[...] = (dot(chosen, high) + dot(chosen, low)).reshape(out.shape)


def score(place, table, turn, own, parts, products, samples, window, cap, sizes):
    depth = parts[0].shape[0] // cap * parts[0].shape[1]
    width = products[0].shape[0] // 2
    devices = sizes[0] * sizes[1]
    return pl.pallas_call(
        functools.partial(score_kernel, sizes, samples, window, cap),
        out_shape=jax.ShapeDtypeStruct((devices, samples // devices, width), jnp.float32),
        in_specs=[SMEM, SMEM, SMEM] + [VMEM] * (1 + len(parts) + len(products)),
        out_specs=VMEM,
        scratch_shapes=[pltpu.VMEM((len(parts) * cap, depth), jnp.float32)],
        compiler_params=params(16),
        name="score",
    )(place, table, turn, own, *parts, *products)


def body(hidden_in, out_grad, proj_in, proj_out, inverse_fisher, queries, lengths, offsets):
    row_count = lax.axis_size("row")
    col_count = lax.axis_size("col")
    sizes = (row_count, col_count)
    chip_count = col_count // CORES
    row_id = lax.axis_index("row")
    col_id = lax.axis_index("col")
    tok_rows = hidden_in.shape[0]
    samples = lengths.shape[0]
    window = min(samples, CORES * tok_rows // SHORTEST + 1)
    cap = -(-3 * samples // (2 * chip_count))
    place = jnp.stack([row_id, col_id])

    def other_core(x):
        return lax.ppermute(x, "col", [(i, i ^ 1) for i in range(col_count)])

    def along_row(x, step):
        return lax.ppermute(x, "row", [(i, i ^ step) for i in range(row_count)])

    def along_col(x, step):
        return lax.ppermute(x, "col", [(i, i ^ (CORES * step)) for i in range(col_count)])

    own, give = project(place, hidden_in, out_grad, proj_in, proj_out, row_count)
    got = other_core(give)
    table, most, turned = prepare(give, offsets, lengths, queries, sizes, tok_rows)
    pieces = windows(place, offsets, lengths, table, own, got, window, sizes, tok_rows)

    half = inverse_fisher.shape[0] // CORES
    mid = half // 2
    chunks_a = [(True, 0, mid)]
    chunks_b = [(True, mid, mid), (False, 0, half)]
    arrived = [pieces[0]] + [along_row(pieces[d], d) for d in range(1, row_count)]
    head, *product_a = product(place, pieces[0], inverse_fisher, None, turned, chunks_a, chunks_b[0])
    packed, rest = pack(place, table, arrived, product_a[0], samples, cap, sizes)

    def everywhere(packed):
        return [packed] + [along_col(packed, d) for d in range(1, chip_count)]

    parts = everywhere(packed)
    product_b = product(place, packed, inverse_fisher, head, turned, chunks_b)
    products_own, products_other = [*product_a, product_b[0]], [product_b[1]]

    def terms_of(turn, parts):
        others = [other_core(part) for part in parts]
        turn = jnp.reshape(turn, (1,))
        own = own_score(parts, products_own, cap)
        return score(place, table, turn, own, others, products_other, samples, window, cap, sizes)

    score_terms = terms_of(jnp.int32(0), release(parts, product_b[0]))

    def another(state):
        turn, total = state
        packed = lax.dynamic_index_in_dim(rest, turn - 1, 0, False)
        return turn + 1, total + terms_of(turn, everywhere(packed))

    _, score_terms = lax.while_loop(lambda state: state[0] * cap < most[0], another, (jnp.int32(1), score_terms))
    devices = row_count * col_count

    terms = lax.all_to_all(score_terms, ("row", "col"), split_axis=0, concat_axis=0, tiled=True)
    owned_rows = samples // devices
    owned_scores = jnp.sum(terms, axis=0)
    device_id = row_id * col_count + col_id
    owned_lengths = lax.dynamic_slice_in_dim(lengths, device_id * owned_rows, owned_rows, 0)
    return score_scale * owned_scores / owned_lengths.astype(jnp.float32)[:, None]


def solution(mesh):
    in_specs = (
        P(("row", "col"), None),
        P(("row", "col"), None),
        P(),
        P(),
        P("row", "col"),
        P("col", None),
        P(),
        P(),
    )
    out_specs = P(("row", "col"), None)
    return jax.shard_map(body, mesh=mesh, in_specs=in_specs, out_specs=out_specs, check_vma=False)
```

```python
import functools

import jax
import jax.numpy as jnp
from jax import lax
from jax.experimental import pallas as pl
from jax.experimental.pallas import tpu as pltpu
from jax.sharding import PartitionSpec as P

SHORTEST = 32
STEP = 256
MOST, LATER = 1, 64
CORES = 2
VMEM = pl.BlockSpec(memory_space=pltpu.VMEM)
SMEM = pl.BlockSpec(memory_space=pltpu.SMEM)
ANY = pl.BlockSpec(memory_space=pl.ANY)
HBM = pl.BlockSpec(memory_space=pltpu.HBM)

score_scale = 0.0625


def halves(x):
    high = x.astype(jnp.bfloat16)
    low = (x - high.astype(jnp.float32)).astype(jnp.bfloat16)
    return high, low


def dot(left, right):
    return jnp.dot(left, right, preferred_element_type=jnp.float32)


def params(mib):
    return pltpu.CompilerParams(vmem_limit_bytes=mib * 2**20)


def project_kernel(steps, row_count, place, hidden, grad, proj_in, proj_out, own, give, *scratch):
    hidden_v, grad_v, in_v, out_v, sems = scratch
    jobs = []
    for source, weights, left, right, count in (
        (grad, proj_out, grad_v, out_v, steps[0]),
        (hidden, proj_in, hidden_v, in_v, steps[1]),
    ):
        wide = source.shape[1] // count
        job = []
        for i in range(count):
            span = pl.ds(i * wide, wide)
            slot = len(jobs) * steps[0] + i
            a = pltpu.make_async_copy(source.at[:, span], left.at[:, span], sems.at[0, slot])
            b = pltpu.make_async_copy(weights.at[span, :], right.at[span, :], sems.at[1, slot])
            a.start()
            b.start()
            job.append((span, a, b))
        jobs.append((left, right, job))
    tok_rows, rank = hidden.shape[0], proj_in.shape[1]
    band = rank // row_count // CORES
    tall = row_count * band
    mine = place[1] % CORES == 0
    for left, right, job in jobs:
        total = None
        for span, a, b in job:
            a.wait()
            b.wait()
            term = dot(left[:, span], right[span, :])
            total = term if total is None else total + term
        if left is grad_v:
            turned = total.T.reshape(row_count, CORES, band, tok_rows)
            first = turned[:, 0].reshape(tall, tok_rows)
            second = turned[:, 1].reshape(tall, tok_rows)
            for ref, value in ((own, jnp.where(mine, first, second)), (give, jnp.where(mine, second, first))):
                for i in range(tok_rows // rank):
                    ref[i * tall : (i + 1) * tall, :] = value[:, i * rank : (i + 1) * rank]
        else:
            own[tok_rows // rank * tall :, :] = total
            give[tok_rows // rank * tall :, :] = total


def project(place, hidden_in, out_grad, proj_in, proj_out, row_count):
    tok_rows, rank = hidden_in.shape[0], proj_in.shape[1]
    steps = (2, 7)
    tall = tok_rows // rank * (rank // CORES) + tok_rows
    out = jax.ShapeDtypeStruct((tall, rank), jnp.float32)
    return pl.pallas_call(
        functools.partial(project_kernel, steps, row_count),
        out_shape=(out, out),
        in_specs=[SMEM, HBM, HBM, HBM, HBM],
        out_specs=(VMEM, VMEM),
        scratch_shapes=[
            pltpu.VMEM(hidden_in.shape, hidden_in.dtype),
            pltpu.VMEM(out_grad.shape, out_grad.dtype),
            pltpu.VMEM(proj_in.shape, proj_in.dtype),
            pltpu.VMEM(proj_out.shape, proj_out.dtype),
            pltpu.SemaphoreType.DMA((2, sum(steps))),
        ],
        compiler_params=params(53),
        name="project",
    )(place, hidden_in, out_grad, proj_in, proj_out)


def rows_from(core, chunk, half):
    ours, first, _ = chunk
    return pl.multiple_of(jnp.where((core == 0) == ours, first, half + first), STEP)


def prepare_kernel(sizes, slots, after, offsets, lengths, queries, table, most, turned):
    row_count, col_count = sizes
    chips = row_count * col_count // CORES
    begin = lax.broadcasted_iota(jnp.int32, (chips, offsets.shape[1]), 0) * slots
    ended = (offsets[...] + lengths[...] <= begin).astype(jnp.int32).sum(axis=1, keepdims=True)
    begun = (offsets[...] < begin + slots).astype(jnp.int32).sum(axis=1, keepdims=True)
    lanes = lax.broadcasted_iota(jnp.int32, (chips, 2 * LATER), 1)
    met = jnp.sum((begun - ended).reshape(row_count, chips // row_count, 1), axis=0)
    most[0] = jnp.max(met)
    table[...] = jnp.where(lanes < LATER, jnp.where(lanes == MOST, jnp.max(met), ended), begun)
    high, low = halves(queries[...].T)
    width = high.shape[0]
    turned[:width, :] = high
    turned[width:, :] = low


def prepare(after, offsets, lengths, queries, sizes, tok_rows):
    depth, width = queries.shape
    chips = sizes[0] * sizes[1] // CORES
    return pl.pallas_call(
        functools.partial(prepare_kernel, sizes, CORES * tok_rows),
        out_shape=(
            jax.ShapeDtypeStruct((chips, 2 * LATER), jnp.int32),
            jax.ShapeDtypeStruct((1,), jnp.int32),
            jax.ShapeDtypeStruct((2 * width, depth), jnp.bfloat16),
        ),
        in_specs=[ANY, VMEM, VMEM, VMEM],
        out_specs=(VMEM, SMEM, VMEM),
        compiler_params=params(16),
        cost_estimate=pl.CostEstimate(flops=depth * width * 2048, bytes_accessed=8 * depth * width, transcendentals=0),
        name="prepare",
    )(after, offsets[None, :], lengths[None, :], queries)


def window_kernel(window, sizes, tok_rows, place, offsets, lengths, table, own, got, *refs):
    row_count, col_count = sizes
    outs, left = refs[:row_count], refs[row_count]
    device = place[0] * col_count + place[1]
    first_sample = jnp.minimum(table[device // CORES, 0], lengths.shape[0] - window)
    rank = own.shape[1]
    strips = tok_rows // rank
    tall = (own.shape[0] - tok_rows) // strips
    pieces = [ref[i * tall : (i + 1) * tall, :] for ref in (own, got) for i in range(strips)]
    grads_high, grads_low = halves(jnp.concatenate(pieces, axis=1))
    high, low = halves(jnp.concatenate([own[strips * tall :, :], got[strips * tall :, :]], axis=0))
    tokens = jnp.concatenate([high, low], axis=1)
    lanes = lax.broadcasted_iota(jnp.int32, (1, 2 * tok_rows), 1)
    other = device + 1 - 2 * (place[1] % CORES)
    positions = jnp.where(lanes < tok_rows, device * tok_rows + lanes, (other - 1) * tok_rows + lanes)
    both = jnp.concatenate([grads_high, grads_low], axis=0)
    for w in range(window):
        begin = offsets[first_sample + w]
        inside = (positions >= begin) & (positions < begin + lengths[first_sample + w])
        left[w * 2 * tall : (w + 1) * 2 * tall, :] = both * inside.astype(jnp.bfloat16)
    sums = dot(left[...], tokens)
    band = tall // row_count
    sums = sums.reshape(window, 2, row_count, band, 2 * rank)
    sums = sums[:, 0, :, :, :rank] + (sums[:, 0, :, :, rank:] + sums[:, 1, :, :, :rank])
    for r in range(row_count):
        step = place[0] ^ r
        for s in range(row_count):

            @pl.when(step == s)
            def _():
                outs[s][...] = sums[:, r]


def windows(place, offsets, lengths, table, own, got, window, sizes, tok_rows):
    rank = own.shape[1]
    tall = (own.shape[0] - tok_rows) // (tok_rows // rank)
    out = jax.ShapeDtypeStruct((window, tall // sizes[0], rank), jnp.float32)
    return pl.pallas_call(
        functools.partial(window_kernel, window, sizes, tok_rows),
        out_shape=(out,) * sizes[0],
        in_specs=[SMEM, SMEM, SMEM, SMEM, VMEM, VMEM],
        out_specs=(VMEM,) * sizes[0],
        scratch_shapes=[pltpu.VMEM((window * 2 * tall, 2 * tok_rows), jnp.bfloat16)],
        compiler_params=params(34),
        cost_estimate=pl.CostEstimate(
            flops=16 * window * tall * tok_rows * rank, bytes_accessed=8 * window * tall * rank, transcendentals=0
        ),
        name="windows",
    )(place, offsets, lengths, table, own, got)


def runs(place, table, sizes, step, samples, window):
    row_count, col_count = sizes
    chip, base, found = (place[1] // CORES) ^ step, 0, []
    for d in range(row_count):
        at = (place[0] ^ d) * (col_count // CORES) + chip
        first = table[at, 0]
        count = jnp.minimum(table[at, LATER] - first, window)
        found.append((first, count, first - jnp.minimum(first, samples - window), base))
        base = base + count
    return found


def pack_kernel(sizes, samples, cap, place, table, *refs):
    pieces, (first, rest, total) = refs[: sizes[0]], refs[sizes[0] + 1 :]
    window, band, rank = pieces[0].shape
    total[...] = jnp.zeros_like(total)
    for piece, (_, count, skip, base) in zip(pieces, runs(place, table, sizes, 0, samples, window)):

        def move(i, carry):
            total[base + i] = piece[skip + i]
            return carry

        lax.fori_loop(0, count, move, 0)
    rows = total.reshape(total.shape[0] * band, rank)
    for a in range(band):
        first[a * cap : (a + 1) * cap, :] = rows[pl.ds(a, cap, stride=band), :]
    for k in range(rest.shape[0]):

        @pl.when(table[0, MOST] > (k + 1) * cap)
        def _():
            for a in range(band):
                rest[k, a * cap : (a + 1) * cap, :] = rows[pl.ds((k + 1) * cap * band + a, cap, stride=band), :]


def pack(place, table, pieces, after, samples, cap, sizes):
    window, band, rank = pieces[0].shape
    rounds = -(-len(pieces) * window // cap)
    return pl.pallas_call(
        functools.partial(pack_kernel, sizes, samples, cap),
        out_shape=(
            jax.ShapeDtypeStruct((band * cap, rank), jnp.float32),
            jax.ShapeDtypeStruct((max(rounds - 1, 1), band * cap, rank), jnp.float32),
        ),
        in_specs=[SMEM, SMEM] + [VMEM] * len(pieces) + [ANY],
        out_specs=(VMEM, VMEM),
        scratch_shapes=[pltpu.VMEM((max(rounds, 2) * cap, band, rank), jnp.float32)],
        compiler_params=params(16),
        name="pack",
    )(place, table, *pieces, after)


def release_kernel(*refs):
    pass


def release(parts, after):
    return pl.pallas_call(
        release_kernel,
        out_shape=tuple(jax.ShapeDtypeStruct(part.shape, part.dtype) for part in parts),
        in_specs=[ANY] * (len(parts) + 1),
        out_specs=(ANY,) * len(parts),
        input_output_aliases={i + 1: i for i in range(len(parts))},
        compiler_params=params(16),
        name="release",
    )(after, *parts)


def across(left, right):
    return lax.dot_general(left, right, (((1,), (1,)), ((), ())), preferred_element_type=jnp.float32)


def product_kernel(chunks, later, half, place, after, fisher, turned, *refs):
    count = len(chunks) + (1 if later else 0)
    heads, outs, (fisher_v, split, sems) = refs[: -3 - count], refs[-3 - count : -3], refs[-3:]
    core = place[1] % CORES
    early = [ref.at[pl.ds(i, STEP), :] for ref in heads for i in range(0, ref.shape[0], STEP)]
    ready = len(early) * STEP
    width = turned.shape[0] // 2
    copies, at = [], 0
    for chunk in chunks:
        source = rows_from(core, chunk, half)
        for step in range(0, chunk[2], STEP):
            if at >= ready:
                copy = pltpu.make_async_copy(
                    fisher.at[pl.ds(source + step, STEP), :],
                    fisher_v.at[pl.ds(at - ready, STEP), :],
                    sems.at[1 + at // STEP],
                )
                copy.start()
                copies.append(copy)
            else:
                copies.append(None)
            at += STEP
    if later:
        coming, outs = outs[0], outs[1:]
        source = rows_from(core, later, half)
        ahead = pltpu.make_async_copy(fisher.at[pl.ds(source, coming.shape[0]), :], coming, sems.at[0])
        ahead.start()
    at = 0
    for out, (_, _, rows) in zip(outs, chunks):
        for begin in range(0, rows, split.shape[1]):
            size = min(split.shape[1], rows - begin)
            for step in range(0, size, STEP):
                if copies[at // STEP] is None:
                    piece = early[at // STEP][...]
                else:
                    copies[at // STEP].wait()
                    piece = fisher_v[at - ready : at - ready + STEP, :]
                split[0, step : step + STEP, :], split[1, step : step + STEP, :] = halves(piece)
                at += STEP
            term = across(turned[...], split[0, :size, :])
            term = term[:width] + (term[width:] + across(turned[:width, :], split[1, :size, :]))
            span = slice(begin, begin + size)
            out[:width, span], out[width:, span] = halves(term)
    if later:
        ahead.wait()


def product(place, after, inverse_fisher, heads, turned, chunks, later=None):
    width = turned.shape[0] // 2
    depth = inverse_fisher.shape[1]
    out_shape = [jax.ShapeDtypeStruct((2 * STEP, depth), jnp.float32)] if later else []
    out_shape += [jax.ShapeDtypeStruct((2 * width, chunk[2]), jnp.bfloat16) for chunk in chunks]
    rows = sum(chunk[2] for chunk in chunks)
    half = inverse_fisher.shape[0] // CORES
    return pl.pallas_call(
        functools.partial(product_kernel, chunks, later, half),
        out_shape=tuple(out_shape),
        in_specs=[SMEM, ANY, HBM, VMEM] + [VMEM] * len(heads),
        out_specs=(VMEM,) * len(out_shape),
        scratch_shapes=[
            pltpu.VMEM((rows - sum(h.shape[0] for h in heads), depth), jnp.float32),
            pltpu.VMEM((2, 2 * STEP, depth), jnp.bfloat16),
            pltpu.SemaphoreType.DMA((1 + rows // STEP,)),
        ],
        compiler_params=params(34),
        cost_estimate=pl.CostEstimate(
            flops=6 * rows * depth * width, bytes_accessed=4 * rows * depth, transcendentals=0
        ),
        name="product",
    )(place, after, inverse_fisher, turned, *heads)


def rows_times(parts, products, left, cap):
    rank = parts[0].shape[1]
    for i, part in enumerate(parts):
        for a in range(part.shape[0] // cap):
            left[i * cap : (i + 1) * cap, a * rank : (a + 1) * rank] = part[a * cap : (a + 1) * cap, :]
    slots = left.shape[0]
    total, at = None, 0
    for ref in products:
        width, depth = ref.shape[0] // 2, ref.shape[1]
        high, low = halves(left[:, at : at + depth])
        term = across(jnp.concatenate([high, low], axis=0), ref[:width, :])
        term = term[:slots] + (term[slots:] + across(high, ref[width:, :]))
        total = term if total is None else total + term
        at += depth
    return total


def own_score_kernel(sizes, samples, window, cap, place, table, turn, *refs):
    chip_count = sizes[1] // CORES
    out, out_held, left = refs[-3:]
    out[...] = rows_times(refs[:chip_count], refs[chip_count:-3], left, cap)
    slots = chip_count * cap
    lanes = lax.broadcasted_iota(jnp.int32, (1, slots), 1)
    held = jnp.full((1, slots), -1, jnp.int32)
    for step in range(chip_count):
        at = lanes - step * cap
        here = (at >= 0) & (at < cap)
        at = at + turn[0] * cap
        for first, count, _, base in runs(place, table, sizes, step, samples, window):
            held = jnp.where(here & (at >= base) & (at < base + count), first + at - base, held)
    out_held[...] = jnp.broadcast_to(held, out_held.shape)


def own_score(place, table, turn, parts, products, samples, window, cap, sizes):
    depth = parts[0].shape[0] // cap * parts[0].shape[1]
    rows, width = len(parts) * cap, products[0].shape[0] // 2
    return pl.pallas_call(
        functools.partial(own_score_kernel, sizes, samples, window, cap),
        out_shape=(jax.ShapeDtypeStruct((rows, width), jnp.float32), jax.ShapeDtypeStruct((8, rows), jnp.int32)),
        in_specs=[SMEM, SMEM, SMEM] + [VMEM] * (len(parts) + len(products)),
        out_specs=(VMEM, VMEM),
        scratch_shapes=[pltpu.VMEM((rows, depth), jnp.float32)],
        compiler_params=params(16),
        cost_estimate=pl.CostEstimate(
            flops=64 * rows * depth * width, bytes_accessed=4 * depth * width, transcendentals=0
        ),
        name="own_score",
    )(place, table, turn, *parts, *products)


def score_kernel(chip_count, samples, cap, own, held, *refs):
    out, left = refs[-2:]
    total = own[...] + rows_times(refs[:chip_count], refs[chip_count:-2], left, cap)
    slots = chip_count * cap
    hit = lax.broadcasted_iota(jnp.int32, (samples, slots), 0) == held[:1, :]
    chosen = hit.astype(jnp.bfloat16)
    high, low = halves(total)
    out[...] = (dot(chosen, high) + dot(chosen, low)).reshape(out.shape)


def score(own, held, parts, products, samples, cap, sizes):
    depth = parts[0].shape[0] // cap * parts[0].shape[1]
    width = products[0].shape[0] // 2
    devices = sizes[0] * sizes[1]
    return pl.pallas_call(
        functools.partial(score_kernel, len(parts), samples, cap),
        out_shape=jax.ShapeDtypeStruct((devices, samples // devices, width), jnp.float32),
        in_specs=[VMEM] * (2 + len(parts) + len(products)),
        out_specs=VMEM,
        scratch_shapes=[pltpu.VMEM((len(parts) * cap, depth), jnp.float32)],
        compiler_params=params(16),
        name="score",
    )(own, held, *parts, *products)


def body(hidden_in, out_grad, proj_in, proj_out, inverse_fisher, queries, lengths, offsets):
    row_count = lax.axis_size("row")
    col_count = lax.axis_size("col")
    sizes = (row_count, col_count)
    chip_count = col_count // CORES
    row_id = lax.axis_index("row")
    col_id = lax.axis_index("col")
    tok_rows = hidden_in.shape[0]
    samples = lengths.shape[0]
    window = min(samples, CORES * tok_rows // SHORTEST + 1)
    cap = -(-3 * samples // (2 * chip_count))
    place = jnp.stack([row_id, col_id])

    def other_core(x):
        return lax.ppermute(x, "col", [(i, i ^ 1) for i in range(col_count)])

    def along_row(x, step):
        return lax.ppermute(x, "row", [(i, i ^ step) for i in range(row_count)])

    def along_col(x, step):
        return lax.ppermute(x, "col", [(i, i ^ (CORES * step)) for i in range(col_count)])

    own, give = project(place, hidden_in, out_grad, proj_in, proj_out, row_count)
    got = other_core(give)
    half = inverse_fisher.shape[0] // CORES
    mid = half // 2
    chunks_a = [(True, 0, mid)]
    chunks_b = [(True, mid, mid), (False, 0, half)]
    table, most, turned = prepare(give, offsets, lengths, queries, sizes, tok_rows)
    pieces = windows(place, offsets, lengths, table, own, got, window, sizes, tok_rows)

    arrived = [pieces[0]] + [along_row(pieces[d], d) for d in range(1, row_count)]
    head, *product_a = product(place, pieces[0], inverse_fisher, [], turned, chunks_a, chunks_b[0])
    packed, rest = pack(place, table, arrived, product_a[0], samples, cap, sizes)

    def everywhere(packed):
        return [packed] + [along_col(packed, d) for d in range(1, chip_count)]

    parts = everywhere(packed)
    product_b = product(place, packed, inverse_fisher, [head], turned, chunks_b)
    products_own, products_other = [*product_a, product_b[0]], [product_b[1]]

    def terms_of(turn, parts, other):
        others = [other] + [other_core(part) for part in parts[1:]]
        turn = jnp.reshape(turn, (1,))
        own, held = own_score(place, table, turn, parts, products_own, samples, window, cap, sizes)
        return score(own, held, others, products_other, samples, cap, sizes)

    parts = release(parts, product_b[0])
    score_terms = terms_of(jnp.int32(0), parts, other_core(parts[0]))

    def another(state):
        turn, total = state
        packed = lax.dynamic_index_in_dim(rest, turn - 1, 0, False)
        return turn + 1, total + terms_of(turn, everywhere(packed), other_core(packed))

    _, score_terms = lax.while_loop(lambda state: state[0] * cap < most[0], another, (jnp.int32(1), score_terms))
    devices = row_count * col_count

    terms = lax.all_to_all(score_terms, ("row", "col"), split_axis=0, concat_axis=0, tiled=True)
    owned_rows = samples // devices
    owned_scores = jnp.sum(terms, axis=0)
    device_id = row_id * col_count + col_id
    owned_lengths = lax.dynamic_slice_in_dim(lengths, device_id * owned_rows, owned_rows, 0)
    return score_scale * owned_scores / owned_lengths.astype(jnp.float32)[:, None]


def solution(mesh):
    in_specs = (
        P(("row", "col"), None),
        P(("row", "col"), None),
        P(),
        P(),
        P("row", "col"),
        P("col", None),
        P(),
        P(),
    )
    out_specs = P(("row", "col"), None)
    return jax.shard_map(body, mesh=mesh, in_specs=in_specs, out_specs=out_specs, check_vma=False)
```
